32 devices in a mesh: group: 2 (over y), fsdp: 4 (over z), tensor: 4 (over x, core).
Axes of the slice: x: 2, y: 2, z: 4, core: 2. Of those that a mesh axis runs over, the one named last changes fastest.
Arguments:
- inputs: bfloat16 [1536, 8192], P(('group', 'fsdp'), 'tensor'), parts along dimension 0, may hold values from -3 to 3
- grad_out: bfloat16 [1536, 28672], P(('group', 'tensor'), 'fsdp'), parts along dimension 0, may hold values from -6 to 6
- base_weight: bfloat16 [8192, 28672], P('tensor', 'fsdp'), may hold values from -0.03125 to 0.03125
- factor_a: bfloat16 [6, 8192, 64], P(None, ('tensor', 'fsdp')), may hold values from -0.1875 to 0.1875
- factor_b: bfloat16 [6, 64, 28672], P(None, None, 'fsdp'), may hold values from -0.03125 to 0.03125
- group_adapter: int32 [16], P('group'), parts along dimension 0, may hold values from 0 to 5
- group_len: int32 [16], P('group'), parts along dimension 0, may hold values from 1 to 96, 576 in all
Outputs:
- input_grad: bfloat16 [1536, 8192], P(('group', 'fsdp'), 'tensor'), parts along dimension 0
- grad_a: float32 [12, 8192, 64], P('group', ('tensor', 'fsdp')), parts along dimension 0
- grad_b: bfloat16 [12, 64, 28672], P('group', None, 'fsdp'), parts along dimension 0
The draws below stay inside these ranges and needn't reach their ends.
There are 2 independent parts, one for each index of `group`. The reference program is written for one: setup_inputs(seed, part) draws one part's arguments, and reference() takes and returns one part's arrays. A program takes and returns all parts, laid end to end along the dimension named above; an argument that names none is the same for every part. Nothing has to cross between parts.
Inputs may be any that keep to these rules, and one draw needn't show every extreme that they name: `group_adapter`: group g is hosted by index g // 2 of fsdp; an adapter may have several groups. `group_len`: rows of a group past its length are padding; some group is full.
All inputs are finite; a program needn't handle non-finite values.
Results may differ from the reference program's by a relative error of at most 0.011.
Values may be sent and summed in bfloat16 or wider, within the bound.
A program may use at most 128 MiB of HBM per device.

```python
import math
import jax
import jax.numpy as jnp
import numpy as np
from jax import lax

D = 8192
FW = 28672
R = 64
ADAPTERS = 6
TOKENS = 768
NGROUPS = 8
SLOT = 96
N_FSDP = 4


def with_ends(result, own_key, least, high):
    shape = result.shape
    index_at = [jax.random.randint(jax.random.fold_in(own_key, axis), (), 0, shape[axis]) for axis in range(len(shape))]
    result = result.at[tuple(index_at)].set(least)
    longest = shape.index(max(shape))
    index_at[longest] = (index_at[longest] + 1) % shape[longest]
    return result.at[tuple(index_at)].set(high)


def raised(result, own_key, source, target, shards_of, factor):
    owner, partner = [(jnp.arange(result.shape[dim]) // (result.shape[dim] // shards_of)).reshape([-1 if axis == dim else 1 for axis in range(result.ndim)]) for dim in (source, target)]
    chosen = jax.random.permutation(own_key, shards_of)[partner]
    strong = (owner == chosen) | (owner == (partner + shards_of // 2) % shards_of)
    return jnp.where(strong, factor * result, result)


def block_levels(rng, dims, cuts, least, top_value):
    level = 1.0
    for axis_at, blocks in cuts:
        steps = jax.random.uniform(jax.random.fold_in(jax.random.fold_in(rng, 6), axis_at), (blocks,), jnp.float32, least / len(cuts), top_value / len(cuts))
        level = level * jnp.repeat(jnp.exp(steps), dims[axis_at] // blocks).reshape((-1,) + (1,) * (len(dims) - 1 - axis_at))
    return level


def rank_bounds(amount, slope):
    portions = [(1 << 20) // math.isqrt(rank ** slope) + 1 for rank in range(1, amount + 1)]
    width = 1 + sum(portions) // (1 << 30)
    return np.cumsum(np.array([max(1, weight // width) for weight in portions]))


def ranked_ids(own_key, dims, amount, skew):
    listing = rank_bounds(amount, skew)
    pick = jax.random.randint(jax.random.fold_in(own_key, 1), dims, 0, int(listing[amount - 1]))
    rank = jnp.searchsorted(jnp.asarray(listing, jnp.int32), pick, side="right")
    return jax.random.permutation(jax.random.fold_in(own_key, 2), amount)[rank].astype(jnp.int32)


def length_profile(number_of, total, limit, lean):
    weights = [(1 << 20) // math.isqrt(grade ** lean) + 1 for grade in range(2, number_of + 1)]
    surplus, holding = total - limit - (number_of - 1), [1] * (number_of - 1)
    while surplus > 0:
        movable = [i for i in range(number_of - 1) if holding[i] < limit]
        pool, budget = sum([weights[i] for i in movable]), surplus
        for i in movable:
            extra = min(limit - holding[i], max(1, budget * weights[i] // pool), surplus)
            holding[i] = holding[i] + extra
            surplus = surplus - extra
    return np.array([limit] + holding)


def uneven(key, count, total, reach, slope):
    if count == 2:
        one = jax.random.randint(key, (), max(1, total - reach), min(reach, total - 1) + 1)
        return jnp.stack([one, total - one])
    tallies = jnp.asarray(length_profile(count, total, reach, slope), jnp.int32)
    couples = (count - 1) // 2
    giver, receiver = tallies[1:1 + 2 * couples:2], tallies[2:2 + 2 * couples:2]
    margin = jnp.minimum(giver - 1, reach - receiver)
    shifted = jax.random.randint(jax.random.fold_in(key, 1), (couples,), 0, 1 << 20) % (margin + 1)
    tallies = tallies.at[1:1 + 2 * couples:2].set(giver - shifted).at[2:2 + 2 * couples:2].set(receiver + shifted)
    return tallies[jax.random.permutation(jax.random.fold_in(key, 2), count)]


def bell_draw(stream_key, extent, scale, reach, pieces=(), held_as=jnp.bfloat16):
    array = scale * jax.random.normal(stream_key, extent, jnp.float32)
    if pieces:
        array = array * block_levels(stream_key, extent, pieces, -0.22, 0.18)
    return jnp.clip(array, -reach, reach).astype(held_as)


def bell_draw_with(rng, shape, deviation, reach, cuts, heavy, kind=jnp.bfloat16):
    entries = deviation * jax.random.normal(rng, shape, jnp.float32)
    if cuts:
        entries = entries * block_levels(rng, shape, cuts, -0.22, 0.18)
    return jnp.clip(raised(entries, jax.random.fold_in(rng, 3), *heavy), -reach, reach).astype(kind)


def setup_inputs(seed: int = 0, part: int = 0) -> dict:
    streams_of = jax.random.split(jax.random.key(seed), 8)
    part_keys = jax.random.split(jax.random.fold_in(streams_of[7], part), 8)
    inputs = bell_draw(part_keys[0], (TOKENS, D), 0.5, 3.0, ((0, 4), (1, 4)))
    grad_out = bell_draw_with(part_keys[1], (TOKENS, FW), 1.0, 6.0, ((0, 4), (1, 4)), (1, 0, 4, 2.0))
    base_weight = bell_draw(streams_of[2], (D, FW), FW ** -0.5, 0.03125, ((0, 4), (1, 4)))
    factor_a = bell_draw(streams_of[3], (ADAPTERS, D, R), (D // 8) ** -0.5, 0.1875, ((1, 16),))
    factor_b = bell_draw(streams_of[4], (ADAPTERS, R, FW), FW ** -0.5, 0.03125, ((2, 4),))
    group_adapter = with_ends(ranked_ids(part_keys[5], (NGROUPS,), ADAPTERS, 2), jax.random.fold_in(part_keys[5], 3), 0, ADAPTERS - 1).astype(jnp.int32)
    group_len = uneven(part_keys[6], NGROUPS, 3 * TOKENS // 4, SLOT, 2).astype(jnp.int32)
    return dict(inputs=inputs, grad_out=grad_out, base_weight=base_weight, factor_a=factor_a, factor_b=factor_b, group_adapter=group_adapter, group_len=group_len)


def reference(inputs, grad_out, base_weight, factor_a, factor_b, group_adapter, group_len):
    total_rows = inputs.shape[0]
    adapters = factor_a.shape[0]
    slot_rows = total_rows // group_adapter.shape[0]
    row_index = jnp.arange(total_rows, dtype=jnp.int32)
    adapter_row = jnp.repeat(group_adapter, slot_rows)
    length_row = jnp.repeat(group_len, slot_rows)
    row_valid = (row_index % slot_rows < length_row).astype(jnp.float32)
    member = (adapter_row[:, None] == jnp.arange(adapters, dtype=jnp.int32)[None, :]).astype(jnp.float32) * row_valid[:, None]
    block_cols = FW // N_FSDP

    def add_block(running, block_index):
        start_col = (block_index * block_cols).astype(jnp.int32)
        grad_piece = lax.dynamic_slice_in_dim(grad_out, start_col, block_cols, 1)
        weight_piece = lax.dynamic_slice_in_dim(base_weight, start_col, block_cols, 1)
        block_term = lax.dot_general(grad_piece, weight_piece, (((1,), (1,)), ((), ())), preferred_element_type=jnp.float32)
        return running + block_term, None

    base_term, _ = lax.scan(add_block, jnp.zeros((total_rows, D), jnp.float32), jnp.arange(N_FSDP, dtype=jnp.int32))
    b_flat = factor_b.reshape(adapters * R, FW)
    grad_every = lax.dot_general(grad_out, b_flat, (((1,), (1,)), ((), ())), preferred_element_type=jnp.float32)
    low_grad = jnp.sum(grad_every.reshape(total_rows, adapters, R) * member[:, :, None], axis=1)
    a_flat = jnp.transpose(factor_a, (1, 0, 2)).reshape(D, adapters * R)
    input_every = jnp.dot(inputs, a_flat, preferred_element_type=jnp.float32)
    low_in = jnp.sum(input_every.reshape(total_rows, adapters, R) * member[:, :, None], axis=1)
    low_grad_b = low_grad.astype(jnp.bfloat16)
    low_in_b = low_in.astype(jnp.bfloat16)
    spread_grad = (member[:, :, None] * low_grad_b.astype(jnp.float32)[:, None, :]).reshape(total_rows, adapters * R).astype(jnp.bfloat16)
    spread_in = (member[:, :, None] * low_in_b.astype(jnp.float32)[:, None, :]).reshape(total_rows, adapters * R).astype(jnp.bfloat16)
    low_rank = lax.dot_general(spread_grad, a_flat, (((1,), (1,)), ((), ())), preferred_element_type=jnp.float32)
    input_grad = (base_term + low_rank).astype(jnp.bfloat16)
    grad_flat = lax.dot_general(inputs, spread_grad, (((0,), (0,)), ((), ())), preferred_element_type=jnp.float32)
    grad_a = jnp.transpose(grad_flat.reshape(D, adapters, R), (1, 0, 2))
    grad_b = lax.dot_general(spread_in, grad_out, (((0,), (0,)), ((), ())), preferred_element_type=jnp.float32)
    grad_b = grad_b.reshape(adapters, R, FW).astype(jnp.bfloat16)
    return input_grad, grad_a, grad_b
```

```python
import jax
import jax.numpy as jnp
from jax import lax
from jax.sharding import PartitionSpec as P

def body(inputs, grad_out, base_weight, factor_a, factor_b, group_adapter, group_len):
    host_rows, feature_cols = inputs.shape
    GPD = group_adapter.shape[0] // lax.axis_size("fsdp")
    slot_rows = host_rows // GPD
    owner_index = lax.axis_index("fsdp")
    adapters = factor_b.shape[0]
    rank_dim = factor_b.shape[1]
    hidden_cols = factor_b.shape[2]
    gathered = lax.all_gather(grad_out, "tensor", axis=0, tiled=True)
    total_rows = gathered.shape[0]
    row_index = jnp.arange(total_rows, dtype=jnp.int32)
    adapter_row = jnp.repeat(group_adapter, slot_rows)
    length_row = jnp.repeat(group_len, slot_rows)
    row_valid = (row_index % slot_rows < length_row).astype(jnp.float32)
    member = (adapter_row[:, None] == jnp.arange(adapters, dtype=jnp.int32)[None, :]).astype(
        jnp.float32
    ) * row_valid[:, None]
    b_flat = factor_b.reshape(adapters * rank_dim, hidden_cols)
    grad_every = lax.dot_general(
        gathered, b_flat, (((1,), (1,)), ((), ())), preferred_element_type=jnp.float32
    )
    grad_part = jnp.sum(
        grad_every.reshape(total_rows, adapters, rank_dim) * member[:, :, None], axis=1
    )
    low_grad = lax.psum_scatter(grad_part, "fsdp", scatter_dimension=0, tiled=True)
    base_term = lax.psum_scatter(
        lax.dot_general(
            gathered, base_weight, (((1,), (1,)), ((), ())), preferred_element_type=jnp.float32
        ),
        "fsdp",
        scatter_dimension=0,
        tiled=True,
    )
    host_list = lax.dynamic_slice_in_dim(group_adapter, owner_index * GPD, GPD)
    host_member = host_list[:, None] == jnp.arange(adapters, dtype=jnp.int32)[None, :]
    host_pick = host_member.astype(jnp.bfloat16)
    picked = jnp.einsum(
        "ga,adr->gdr",
        host_pick,
        lax.all_gather(factor_a, "fsdp", axis=1, tiled=True),
        preferred_element_type=jnp.float32,
    ).astype(jnp.bfloat16)
    input_groups = inputs.reshape(GPD, slot_rows, feature_cols)
    input_part = jnp.einsum(
        "gsd,gdr->gsr", input_groups, picked, preferred_element_type=jnp.float32
    )
    low_in = lax.psum(input_part, "tensor")
    host_valid = lax.dynamic_slice_in_dim(row_valid, owner_index * host_rows, host_rows).reshape(
        GPD, slot_rows
    )
    low_in_b = (low_in * host_valid[:, :, None]).astype(jnp.bfloat16)
    low_grad_b = low_grad.astype(jnp.bfloat16).reshape(GPD, slot_rows, rank_dim)
    low_rank = jnp.einsum("gsr,gdr->gsd", low_grad_b, picked, preferred_element_type=jnp.float32)
    input_grad = (base_term + low_rank.reshape(host_rows, feature_cols)).astype(jnp.bfloat16)
    host_grad = jnp.einsum(
        "gsd,gsr->gdr", input_groups, low_grad_b, preferred_element_type=jnp.float32
    )
    spread_grad = jnp.einsum(
        "ga,gdr->adr", host_member.astype(jnp.float32), host_grad, precision=lax.Precision.HIGHEST
    )
    grad_a = lax.psum_scatter(spread_grad, "fsdp", scatter_dimension=1, tiled=True)
    all_inputs = lax.all_gather(low_in_b.reshape(host_rows, rank_dim), "fsdp", axis=0, tiled=True)
    spread_in = (member.astype(jnp.bfloat16)[:, :, None] * all_inputs[:, None, :]).reshape(
        total_rows, adapters * rank_dim
    )
    grad_flat = lax.dot_general(
        spread_in, gathered, (((0,), (0,)), ((), ())), preferred_element_type=jnp.float32
    )
    grad_b = grad_flat.reshape(adapters, rank_dim, hidden_cols).astype(jnp.bfloat16)
    return (input_grad, grad_a, grad_b)


def take(blocks, index):
    return lax.dynamic_index_in_dim(blocks, index, 0, keepdims=False)


def swap(value, axis, mask, count):
    return lax.ppermute(value, axis, [(i, i ^ mask) for i in range(count)])


def after(value, earlier):
    return lax.optimization_barrier((value, earlier))[0]


def body4(inputs, grad_out, base_weight, factor_a, factor_b, group_adapter, group_len):
    n = 4
    host_rows, feature_cols = inputs.shape
    adapters, rank_dim, hidden_cols = factor_b.shape
    own_cols = feature_cols // n
    total_rows = host_rows * n
    slot_rows = total_rows // group_adapter.shape[0]
    t = lax.axis_index("tensor")
    z = lax.axis_index("fsdp")
    wide = adapters * rank_dim
    chunks = 2
    step_rows = host_rows // chunks
    bf16, f32 = jnp.bfloat16, jnp.float32

    mate = swap(grad_out, "tensor", 1, n)
    pieces = []
    across = None
    for c in range(chunks):
        sent = grad_out[c * step_rows : (c + 1) * step_rows]
        if across is not None:
            sent = after(sent, across)
        across = swap(sent, "tensor", 2, n)
        relayed = swap(across, "tensor", 1, n)
        pieces.append((c, across, relayed))

    by_owner = inputs.reshape(host_rows, n, own_cols).transpose(1, 0, 2)
    kept = take(by_owner, z)
    arrived = [kept] + [swap(take(by_owner, z ^ j), "fsdp", j, n) for j in range(1, n)]
    rows_in = jnp.stack(arrived)

    row_index = jnp.arange(total_rows, dtype=jnp.int32)
    adapter_row = jnp.repeat(group_adapter, slot_rows)
    length_row = jnp.repeat(group_len, slot_rows)
    row_valid = (row_index % slot_rows < length_row).astype(f32)
    member = (adapter_row[:, None] == jnp.arange(adapters, dtype=jnp.int32)[None, :]).astype(
        f32
    ) * row_valid[:, None]
    member_blocks = member.reshape(n, host_rows, adapters)

    def ordered(blocks, start):
        return jnp.stack([take(blocks, start ^ j) for j in range(n)])

    def pick(every, who):
        rows = every.shape[0]
        return jnp.sum(every.reshape(rows, adapters, rank_dim) * who[:, :, None], axis=1)

    def spread(low, who):
        rows = low.shape[0]
        return (who.astype(bf16)[:, :, None] * low.astype(bf16)[:, None, :]).reshape(rows, wide)

    b_flat = factor_b.reshape(wide, hidden_cols)
    a_flat = jnp.transpose(factor_a, (1, 0, 2)).reshape(own_cols, wide)
    grad_part = pick(
        lax.dot_general(grad_out, b_flat, (((1,), (1,)), ((), ())), preferred_element_type=f32),
        take(member_blocks, t),
    )
    grad_part = lax.dynamic_update_index_in_dim(
        jnp.zeros((n, host_rows, rank_dim), f32), grad_part, t, 0
    ).reshape(total_rows, rank_dim)
    rows_in = ordered(rows_in, z).reshape(total_rows, own_cols)
    in_part = pick(jnp.dot(rows_in, a_flat, preferred_element_type=f32), member)
    low = lax.psum(jnp.concatenate([grad_part, in_part], axis=1), ("tensor", "fsdp"))
    low_grad = low[:, :rank_dim]
    low_in = low[:, rank_dim:]

    spread_grad = spread(low_grad, member)
    grad_a = lax.dot_general(
        spread_grad, rows_in, (((0,), (0,)), ((), ())), preferred_element_type=f32
    ).reshape(adapters, rank_dim, own_cols).transpose(0, 2, 1)
    low_rank = lax.dot_general(
        spread_grad, a_flat, (((1,), (1,)), ((), ())), preferred_element_type=f32
    )
    low_rank = lax.dynamic_update_slice_in_dim(
        jnp.zeros((total_rows, feature_cols), bf16), low_rank.astype(bf16), z * own_cols, 1
    ).reshape(n, host_rows, feature_cols)

    in_order = ordered(low_in.reshape(n, host_rows, rank_dim), t)
    member_order = ordered(member_blocks, t)

    grad_b = None
    finished = []
    for c, across, relayed in pieces:
        rows = slice(c * step_rows, (c + 1) * step_rows)
        gathered = jnp.concatenate([grad_out[rows], mate[rows], across, relayed], axis=0)
        part = lax.dot_general(
            gathered, base_weight, (((1,), (1,)), ((), ())), preferred_element_type=f32
        ).astype(bf16).reshape(n, step_rows, feature_cols)

        def own(dest):
            dest = jnp.clip(dest, 0, n - 1)
            return take(part, dest ^ t).astype(f32) + take(low_rank[:, rows], dest).astype(f32)

        up = down = None
        for k in range(1, n):
            to_up, to_down = own(z + n - k), own(z - n + k)
            if up is not None:
                to_up, to_down = to_up + up.astype(f32), to_down + down.astype(f32)
            up = lax.ppermute(to_up.astype(bf16), "fsdp", [(i, i + 1) for i in range(k)])
            down = lax.ppermute(
                to_down.astype(bf16), "fsdp", [(n - 1 - i, n - 2 - i) for i in range(k)]
            )
        finished.append((own(z) + up.astype(f32) + down.astype(f32)).astype(bf16))

        spread_in = spread(
            in_order[:, rows].reshape(n * step_rows, rank_dim),
            member_order[:, rows].reshape(n * step_rows, adapters),
        )
        term = lax.dot_general(
            spread_in, gathered, (((0,), (0,)), ((), ())), preferred_element_type=f32
        )
        grad_b = term if grad_b is None else grad_b + term
    grad_b = grad_b.astype(bf16).reshape(adapters, rank_dim, hidden_cols)
    return (jnp.concatenate(finished, axis=0), grad_a, grad_b)


def solution(mesh):
    small = mesh.shape["fsdp"] == 4 and mesh.shape["tensor"] == 4
    placed = (
        P(("group", "fsdp"), "tensor"),
        P(("group", "tensor"), "fsdp"),
        P("tensor", "fsdp"),
        P(None, ("tensor", "fsdp"), None),
        P(None, None, "fsdp"),
        P("group"),
        P("group"),
    )
    return jax.shard_map(
        body4 if small else body,
        mesh=mesh,
        in_specs=placed,
        out_specs=(
            P(("group", "fsdp"), "tensor"),
            P("group", ("tensor", "fsdp"), None),
            P("group", None, "fsdp"),
        ),
        check_vma=False,
    )
```

```python
import jax
import jax.numpy as jnp
from jax import lax
from jax.sharding import PartitionSpec as P

def body(inputs, grad_out, base_weight, factor_a, factor_b, group_adapter, group_len):
    host_rows, feature_cols = inputs.shape
    GPD = group_adapter.shape[0] // lax.axis_size("fsdp")
    slot_rows = host_rows // GPD
    owner_index = lax.axis_index("fsdp")
    adapters = factor_b.shape[0]
    rank_dim = factor_b.shape[1]
    hidden_cols = factor_b.shape[2]
    gathered = lax.all_gather(grad_out, "tensor", axis=0, tiled=True)
    total_rows = gathered.shape[0]
    row_index = jnp.arange(total_rows, dtype=jnp.int32)
    adapter_row = jnp.repeat(group_adapter, slot_rows)
    length_row = jnp.repeat(group_len, slot_rows)
    row_valid = (row_index % slot_rows < length_row).astype(jnp.float32)
    member = (adapter_row[:, None] == jnp.arange(adapters, dtype=jnp.int32)[None, :]).astype(
        jnp.float32
    ) * row_valid[:, None]
    b_flat = factor_b.reshape(adapters * rank_dim, hidden_cols)
    grad_every = lax.dot_general(
        gathered, b_flat, (((1,), (1,)), ((), ())), preferred_element_type=jnp.float32
    )
    grad_part = jnp.sum(
        grad_every.reshape(total_rows, adapters, rank_dim) * member[:, :, None], axis=1
    )
    low_grad = lax.psum_scatter(grad_part, "fsdp", scatter_dimension=0, tiled=True)
    base_term = lax.psum_scatter(
        lax.dot_general(
            gathered, base_weight, (((1,), (1,)), ((), ())), preferred_element_type=jnp.float32
        ),
        "fsdp",
        scatter_dimension=0,
        tiled=True,
    )
    host_list = lax.dynamic_slice_in_dim(group_adapter, owner_index * GPD, GPD)
    host_member = host_list[:, None] == jnp.arange(adapters, dtype=jnp.int32)[None, :]
    host_pick = host_member.astype(jnp.bfloat16)
    picked = jnp.einsum(
        "ga,adr->gdr",
        host_pick,
        lax.all_gather(factor_a, "fsdp", axis=1, tiled=True),
        preferred_element_type=jnp.float32,
    ).astype(jnp.bfloat16)
    input_groups = inputs.reshape(GPD, slot_rows, feature_cols)
    input_part = jnp.einsum(
        "gsd,gdr->gsr", input_groups, picked, preferred_element_type=jnp.float32
    )
    low_in = lax.psum(input_part, "tensor")
    host_valid = lax.dynamic_slice_in_dim(row_valid, owner_index * host_rows, host_rows).reshape(
        GPD, slot_rows
    )
    low_in_b = (low_in * host_valid[:, :, None]).astype(jnp.bfloat16)
    low_grad_b = low_grad.astype(jnp.bfloat16).reshape(GPD, slot_rows, rank_dim)
    low_rank = jnp.einsum("gsr,gdr->gsd", low_grad_b, picked, preferred_element_type=jnp.float32)
    input_grad = (base_term + low_rank.reshape(host_rows, feature_cols)).astype(jnp.bfloat16)
    host_grad = jnp.einsum(
        "gsd,gsr->gdr", input_groups, low_grad_b, preferred_element_type=jnp.float32
    )
    spread_grad = jnp.einsum(
        "ga,gdr->adr", host_member.astype(jnp.float32), host_grad, precision=lax.Precision.HIGHEST
    )
    grad_a = lax.psum_scatter(spread_grad, "fsdp", scatter_dimension=1, tiled=True)
    all_inputs = lax.all_gather(low_in_b.reshape(host_rows, rank_dim), "fsdp", axis=0, tiled=True)
    spread_in = (member.astype(jnp.bfloat16)[:, :, None] * all_inputs[:, None, :]).reshape(
        total_rows, adapters * rank_dim
    )
    grad_flat = lax.dot_general(
        spread_in, gathered, (((0,), (0,)), ((), ())), preferred_element_type=jnp.float32
    )
    grad_b = grad_flat.reshape(adapters, rank_dim, hidden_cols).astype(jnp.bfloat16)
    return (input_grad, grad_a, grad_b)


def take(blocks, index):
    return lax.dynamic_index_in_dim(blocks, index, 0, keepdims=False)


def swap(value, axis, mask, count):
    return lax.ppermute(value, axis, [(i, i ^ mask) for i in range(count)])


def after(value, earlier):
    return lax.optimization_barrier((value, earlier))[0]


def body4(inputs, grad_out, base_weight, factor_a, factor_b, group_adapter, group_len):
    n = 4
    host_rows, feature_cols = inputs.shape
    adapters, rank_dim, hidden_cols = factor_b.shape
    own_cols = feature_cols // n
    total_rows = host_rows * n
    slot_rows = total_rows // group_adapter.shape[0]
    t = lax.axis_index("tensor")
    z = lax.axis_index("fsdp")
    wide = adapters * rank_dim
    chunks = 2
    step_rows = host_rows // chunks
    bf16, f32 = jnp.bfloat16, jnp.float32

    mate = swap(grad_out, "tensor", 1, n)
    pieces = []
    across = None
    for c in range(chunks):
        sent = grad_out[c * step_rows : (c + 1) * step_rows]
        if across is not None:
            sent = after(sent, across)
        across = swap(sent, "tensor", 2, n)
        relayed = swap(across, "tensor", 1, n)
        pieces.append((c, across, relayed))

    by_owner = inputs.reshape(host_rows, n, own_cols).transpose(1, 0, 2)
    kept = take(by_owner, z)
    arrived = [kept] + [swap(take(by_owner, z ^ j), "fsdp", j, n) for j in range(1, n)]
    rows_in = jnp.stack(arrived)

    row_index = jnp.arange(total_rows, dtype=jnp.int32)
    adapter_row = jnp.repeat(group_adapter, slot_rows)
    length_row = jnp.repeat(group_len, slot_rows)
    row_valid = (row_index % slot_rows < length_row).astype(f32)
    member = (adapter_row[:, None] == jnp.arange(adapters, dtype=jnp.int32)[None, :]).astype(
        f32
    ) * row_valid[:, None]
    member_blocks = member.reshape(n, host_rows, adapters)

    def ordered(blocks, start):
        return jnp.stack([take(blocks, start ^ j) for j in range(n)])

    def pick(every, who):
        rows = every.shape[0]
        return jnp.sum(every.reshape(rows, adapters, rank_dim) * who[:, :, None], axis=1)

    def spread(low, who):
        rows = low.shape[0]
        return (who.astype(bf16)[:, :, None] * low.astype(bf16)[:, None, :]).reshape(rows, wide)

    b_flat = factor_b.reshape(wide, hidden_cols)
    a_flat = jnp.transpose(factor_a, (1, 0, 2)).reshape(own_cols, wide)
    def doubled(value):
        value = value + swap(value, "fsdp", 1, n)
        return value + swap(value, "fsdp", 2, n)

    def every_block(value):
        pair = jnp.stack([value, swap(value, "tensor", 1, n)])
        return jnp.concatenate([pair, swap(pair, "tensor", 2, n)], axis=0)

    own_member = take(member_blocks, t)
    grad_part = pick(
        lax.dot_general(grad_out, b_flat, (((1,), (1,)), ((), ())), preferred_element_type=f32),
        own_member,
    )
    grad_order = every_block(doubled(grad_part).astype(bf16))
    low_grad = ordered(grad_order, t).reshape(total_rows, rank_dim)

    rows_in = ordered(rows_in, z).reshape(total_rows, own_cols)
    in_part = pick(jnp.dot(rows_in, a_flat, preferred_element_type=f32), member)
    by_core = in_part.reshape(2, 2, host_rows, rank_dim).transpose(1, 0, 2, 3)
    halves = take(by_core, t % 2) + swap(take(by_core, 1 - t % 2), "tensor", 1, n)
    own_in = take(halves, t // 2) + swap(take(halves, 1 - t // 2), "tensor", 2, n)
    in_order = every_block(doubled(own_in).astype(bf16))

    spread_grad = spread(low_grad, member)
    grad_a = lax.dot_general(
        spread_grad, rows_in, (((0,), (0,)), ((), ())), preferred_element_type=f32
    ).reshape(adapters, rank_dim, own_cols).transpose(0, 2, 1)
    low_rank = lax.dot_general(
        spread_grad, a_flat, (((1,), (1,)), ((), ())), preferred_element_type=f32
    )
    low_rank = lax.dynamic_update_slice_in_dim(
        jnp.zeros((total_rows, feature_cols), bf16), low_rank.astype(bf16), z * own_cols, 1
    ).reshape(n, host_rows, feature_cols)

    member_order = ordered(member_blocks, t)

    grad_b = None
    finished = []
    for c, across, relayed in pieces:
        rows = slice(c * step_rows, (c + 1) * step_rows)
        gathered = jnp.concatenate([grad_out[rows], mate[rows], across, relayed], axis=0)
        part = lax.dot_general(
            gathered, base_weight, (((1,), (1,)), ((), ())), preferred_element_type=f32
        ).astype(bf16).reshape(n, step_rows, feature_cols)

        def own(dest):
            dest = jnp.clip(dest, 0, n - 1)
            return take(part, dest ^ t).astype(f32) + take(low_rank[:, rows], dest).astype(f32)

        up = down = None
        for k in range(1, n):
            to_up, to_down = own(z + n - k), own(z - n + k)
            if up is not None:
                to_up, to_down = to_up + up.astype(f32), to_down + down.astype(f32)
            up = lax.ppermute(to_up.astype(bf16), "fsdp", [(i, i + 1) for i in range(k)])
            down = lax.ppermute(
                to_down.astype(bf16), "fsdp", [(n - 1 - i, n - 2 - i) for i in range(k)]
            )
        finished.append((own(z) + up.astype(f32) + down.astype(f32)).astype(bf16))

        spread_in = spread(
            in_order[:, rows].reshape(n * step_rows, rank_dim),
            member_order[:, rows].reshape(n * step_rows, adapters),
        )
        term = lax.dot_general(
            spread_in, gathered, (((0,), (0,)), ((), ())), preferred_element_type=f32
        )
        grad_b = term if grad_b is None else grad_b + term
    grad_b = grad_b.astype(bf16).reshape(adapters, rank_dim, hidden_cols)
    return (jnp.concatenate(finished, axis=0), grad_a, grad_b)


def solution(mesh):
    small = mesh.shape["fsdp"] == 4 and mesh.shape["tensor"] == 4
    placed = (
        P(("group", "fsdp"), "tensor"),
        P(("group", "tensor"), "fsdp"),
        P("tensor", "fsdp"),
        P(None, ("tensor", "fsdp"), None),
        P(None, None, "fsdp"),
        P("group"),
        P("group"),
    )
    return jax.shard_map(
        body4 if small else body,
        mesh=mesh,
        in_specs=placed,
        out_specs=(
            P(("group", "fsdp"), "tensor"),
            P("group", ("tensor", "fsdp"), None),
            P("group", None, "fsdp"),
        ),
        check_vma=False,
    )
```

```python
import jax
import jax.numpy as jnp
from jax import lax
from jax.sharding import PartitionSpec as P

def body(inputs, grad_out, base_weight, factor_a, factor_b, group_adapter, group_len):
    host_rows, feature_cols = inputs.shape
    GPD = group_adapter.shape[0] // lax.axis_size("fsdp")
    slot_rows = host_rows // GPD
    owner_index = lax.axis_index("fsdp")
    adapters = factor_b.shape[0]
    rank_dim = factor_b.shape[1]
    hidden_cols = factor_b.shape[2]
    gathered = lax.all_gather(grad_out, "tensor", axis=0, tiled=True)
    total_rows = gathered.shape[0]
    row_index = jnp.arange(total_rows, dtype=jnp.int32)
    adapter_row = jnp.repeat(group_adapter, slot_rows)
    length_row = jnp.repeat(group_len, slot_rows)
    row_valid = (row_index % slot_rows < length_row).astype(jnp.float32)
    member = (adapter_row[:, None] == jnp.arange(adapters, dtype=jnp.int32)[None, :]).astype(
        jnp.float32
    ) * row_valid[:, None]
    b_flat = factor_b.reshape(adapters * rank_dim, hidden_cols)
    grad_every = lax.dot_general(
        gathered, b_flat, (((1,), (1,)), ((), ())), preferred_element_type=jnp.float32
    )
    grad_part = jnp.sum(
        grad_every.reshape(total_rows, adapters, rank_dim) * member[:, :, None], axis=1
    )
    low_grad = lax.psum_scatter(grad_part, "fsdp", scatter_dimension=0, tiled=True)
    base_term = lax.psum_scatter(
        lax.dot_general(
            gathered, base_weight, (((1,), (1,)), ((), ())), preferred_element_type=jnp.float32
        ),
        "fsdp",
        scatter_dimension=0,
        tiled=True,
    )
    host_list = lax.dynamic_slice_in_dim(group_adapter, owner_index * GPD, GPD)
    host_member = host_list[:, None] == jnp.arange(adapters, dtype=jnp.int32)[None, :]
    host_pick = host_member.astype(jnp.bfloat16)
    picked = jnp.einsum(
        "ga,adr->gdr",
        host_pick,
        lax.all_gather(factor_a, "fsdp", axis=1, tiled=True),
        preferred_element_type=jnp.float32,
    ).astype(jnp.bfloat16)
    input_groups = inputs.reshape(GPD, slot_rows, feature_cols)
    input_part = jnp.einsum(
        "gsd,gdr->gsr", input_groups, picked, preferred_element_type=jnp.float32
    )
    low_in = lax.psum(input_part, "tensor")
    host_valid = lax.dynamic_slice_in_dim(row_valid, owner_index * host_rows, host_rows).reshape(
        GPD, slot_rows
    )
    low_in_b = (low_in * host_valid[:, :, None]).astype(jnp.bfloat16)
    low_grad_b = low_grad.astype(jnp.bfloat16).reshape(GPD, slot_rows, rank_dim)
    low_rank = jnp.einsum("gsr,gdr->gsd", low_grad_b, picked, preferred_element_type=jnp.float32)
    input_grad = (base_term + low_rank.reshape(host_rows, feature_cols)).astype(jnp.bfloat16)
    host_grad = jnp.einsum(
        "gsd,gsr->gdr", input_groups, low_grad_b, preferred_element_type=jnp.float32
    )
    spread_grad = jnp.einsum(
        "ga,gdr->adr", host_member.astype(jnp.float32), host_grad, precision=lax.Precision.HIGHEST
    )
    grad_a = lax.psum_scatter(spread_grad, "fsdp", scatter_dimension=1, tiled=True)
    all_inputs = lax.all_gather(low_in_b.reshape(host_rows, rank_dim), "fsdp", axis=0, tiled=True)
    spread_in = (member.astype(jnp.bfloat16)[:, :, None] * all_inputs[:, None, :]).reshape(
        total_rows, adapters * rank_dim
    )
    grad_flat = lax.dot_general(
        spread_in, gathered, (((0,), (0,)), ((), ())), preferred_element_type=jnp.float32
    )
    grad_b = grad_flat.reshape(adapters, rank_dim, hidden_cols).astype(jnp.bfloat16)
    return (input_grad, grad_a, grad_b)


def take(blocks, index):
    return lax.dynamic_index_in_dim(blocks, index, 0, keepdims=False)


def swap(value, axis, mask, count):
    return lax.ppermute(value, axis, [(i, i ^ mask) for i in range(count)])


def after(value, earlier):
    return lax.optimization_barrier((value, earlier))[0]


def body4(inputs, grad_out, base_weight, factor_a, factor_b, group_adapter, group_len):
    n = 4
    host_rows, feature_cols = inputs.shape
    adapters, rank_dim, hidden_cols = factor_b.shape
    own_cols = feature_cols // n
    total_rows = host_rows * n
    slot_rows = total_rows // group_adapter.shape[0]
    t = lax.axis_index("tensor")
    z = lax.axis_index("fsdp")
    wide = adapters * rank_dim
    chunks = 2
    step_rows = host_rows // chunks
    bf16, f32 = jnp.bfloat16, jnp.float32

    mate = swap(grad_out, "tensor", 1, n)
    legs = 2 * chunks
    leg_rows = host_rows // legs
    across, relayed = [], []
    for c in range(legs):
        sent = grad_out[c * leg_rows : (c + 1) * leg_rows]
        if across:
            sent = after(sent, across[-1])
        across.append(swap(sent, "tensor", 2, n))
        relayed.append(swap(across[-1], "tensor", 1, n))

    by_owner = inputs.reshape(host_rows, n, own_cols).transpose(1, 0, 2)
    kept = take(by_owner, z)
    arrived = [kept] + [swap(take(by_owner, z ^ j), "fsdp", j, n) for j in range(1, n)]
    rows_in = jnp.stack(arrived)

    row_index = jnp.arange(total_rows, dtype=jnp.int32)
    adapter_row = jnp.repeat(group_adapter, slot_rows)
    length_row = jnp.repeat(group_len, slot_rows)
    row_valid = (row_index % slot_rows < length_row).astype(f32)
    member = (adapter_row[:, None] == jnp.arange(adapters, dtype=jnp.int32)[None, :]).astype(
        f32
    ) * row_valid[:, None]
    member_blocks = member.reshape(n, host_rows, adapters)

    def ordered(blocks, start):
        return jnp.stack([take(blocks, start ^ j) for j in range(n)])

    def pick(every, who):
        rows = every.shape[0]
        return jnp.sum(every.reshape(rows, adapters, rank_dim) * who[:, :, None], axis=1)

    def spread(low, who):
        rows = low.shape[0]
        return (who.astype(bf16)[:, :, None] * low.astype(bf16)[:, None, :]).reshape(rows, wide)

    b_flat = factor_b.reshape(wide, hidden_cols)
    a_flat = jnp.transpose(factor_a, (1, 0, 2)).reshape(own_cols, wide)
    def doubled(value):
        value = value + swap(value, "fsdp", 1, n)
        return value + swap(value, "fsdp", 2, n)

    def every_block(value, leg):
        pair = jnp.stack([value, swap(value, "tensor", 1, n)])
        pair = after(pair, across[leg])
        return jnp.concatenate([pair, swap(pair, "tensor", 2, n)], axis=0)

    own_member = take(member_blocks, t)
    grad_part = pick(
        lax.dot_general(grad_out, b_flat, (((1,), (1,)), ((), ())), preferred_element_type=f32),
        own_member,
    )
    grad_order = every_block(doubled(grad_part).astype(bf16), 0)
    low_grad = ordered(grad_order, t).reshape(total_rows, rank_dim)

    rows_in = ordered(rows_in, z).reshape(total_rows, own_cols)
    in_part = pick(jnp.dot(rows_in, a_flat, preferred_element_type=f32), member)
    by_core = in_part.reshape(2, 2, host_rows, rank_dim).transpose(1, 0, 2, 3)
    halves = take(by_core, t % 2) + swap(take(by_core, 1 - t % 2), "tensor", 1, n)
    other = after(take(halves, 1 - t // 2), across[1])
    own_in = take(halves, t // 2) + swap(other, "tensor", 2, n)
    in_order = every_block(doubled(own_in).astype(bf16), 2)

    spread_grad = spread(low_grad, member)
    grad_a = lax.dot_general(
        spread_grad, rows_in, (((0,), (0,)), ((), ())), preferred_element_type=f32
    ).reshape(adapters, rank_dim, own_cols).transpose(0, 2, 1)
    low_rank = lax.dot_general(
        spread_grad, a_flat, (((1,), (1,)), ((), ())), preferred_element_type=f32
    )
    low_rank = lax.dynamic_update_slice_in_dim(
        jnp.zeros((total_rows, feature_cols), bf16), low_rank.astype(bf16), z * own_cols, 1
    ).reshape(n, host_rows, feature_cols)

    member_order = ordered(member_blocks, t)

    grad_b = None
    finished, passed, operands = [], [], []
    for c in range(chunks):
        rows = slice(c * step_rows, (c + 1) * step_rows)
        here = slice(2 * c, 2 * c + 2)
        gathered = jnp.concatenate(
            [grad_out[rows], mate[rows]] + across[here] + relayed[here], axis=0
        )
        if passed:
            gathered = after(gathered, passed[n - 3])
        part = lax.dot_general(
            gathered, base_weight, (((1,), (1,)), ((), ())), preferred_element_type=f32
        ).astype(bf16).reshape(n, step_rows, feature_cols)

        def own(dest):
            dest = jnp.clip(dest, 0, n - 1)
            return take(part, dest ^ t).astype(f32) + take(low_rank[:, rows], dest).astype(f32)

        spread_in = spread(
            in_order[:, rows].reshape(n * step_rows, rank_dim),
            member_order[:, rows].reshape(n * step_rows, adapters),
        )
        operands.append((spread_in, gathered))
        up = down = None
        passed = []
        for k in range(1, n):
            to_up, to_down = own(z + n - k), own(z - n + k)
            if up is not None:
                to_up, to_down = to_up + up.astype(f32), to_down + down.astype(f32)
            up = lax.ppermute(to_up.astype(bf16), "fsdp", [(i, i + 1) for i in range(k)])
            down = lax.ppermute(
                to_down.astype(bf16), "fsdp", [(n - 1 - i, n - 2 - i) for i in range(k)]
            )
            if c == chunks - 1 and k > 1:
                spread_in, gathered = operands[k - 2]
                term = lax.dot_general(
                    after(spread_in, passed[-1]),
                    gathered,
                    (((0,), (0,)), ((), ())),
                    preferred_element_type=f32,
                )
                grad_b = term if grad_b is None else grad_b + term
                if k < n - 1:
                    grad_b, up, down = lax.optimization_barrier((grad_b, up, down))
            passed.append((up, down))
        finished.append((own(z) + up.astype(f32) + down.astype(f32)).astype(bf16))

    grad_b = grad_b.astype(bf16).reshape(adapters, rank_dim, hidden_cols)
    return (jnp.concatenate(finished, axis=0), grad_a, grad_b)


def solution(mesh):
    small = mesh.shape["fsdp"] == 4 and mesh.shape["tensor"] == 4
    placed = (
        P(("group", "fsdp"), "tensor"),
        P(("group", "tensor"), "fsdp"),
        P("tensor", "fsdp"),
        P(None, ("tensor", "fsdp"), None),
        P(None, None, "fsdp"),
        P("group"),
        P("group"),
    )
    return jax.shard_map(
        body4 if small else body,
        mesh=mesh,
        in_specs=placed,
        out_specs=(
            P(("group", "fsdp"), "tensor"),
            P("group", ("tensor", "fsdp"), None),
            P("group", None, "fsdp"),
        ),
        check_vma=False,
    )
```

```python
import jax
import jax.numpy as jnp
from jax import lax
from jax.sharding import PartitionSpec as P

def body(inputs, grad_out, base_weight, factor_a, factor_b, group_adapter, group_len):
    host_rows, feature_cols = inputs.shape
    GPD = group_adapter.shape[0] // lax.axis_size("fsdp")
    slot_rows = host_rows // GPD
    owner_index = lax.axis_index("fsdp")
    adapters = factor_b.shape[0]
    rank_dim = factor_b.shape[1]
    hidden_cols = factor_b.shape[2]
    gathered = lax.all_gather(grad_out, "tensor", axis=0, tiled=True)
    total_rows = gathered.shape[0]
    row_index = jnp.arange(total_rows, dtype=jnp.int32)
    adapter_row = jnp.repeat(group_adapter, slot_rows)
    length_row = jnp.repeat(group_len, slot_rows)
    row_valid = (row_index % slot_rows < length_row).astype(jnp.float32)
    member = (adapter_row[:, None] == jnp.arange(adapters, dtype=jnp.int32)[None, :]).astype(
        jnp.float32
    ) * row_valid[:, None]
    b_flat = factor_b.reshape(adapters * rank_dim, hidden_cols)
    grad_every = lax.dot_general(
        gathered, b_flat, (((1,), (1,)), ((), ())), preferred_element_type=jnp.float32
    )
    grad_part = jnp.sum(
        grad_every.reshape(total_rows, adapters, rank_dim) * member[:, :, None], axis=1
    )
    low_grad = lax.psum_scatter(grad_part, "fsdp", scatter_dimension=0, tiled=True)
    base_term = lax.psum_scatter(
        lax.dot_general(
            gathered, base_weight, (((1,), (1,)), ((), ())), preferred_element_type=jnp.float32
        ),
        "fsdp",
        scatter_dimension=0,
        tiled=True,
    )
    host_list = lax.dynamic_slice_in_dim(group_adapter, owner_index * GPD, GPD)
    host_member = host_list[:, None] == jnp.arange(adapters, dtype=jnp.int32)[None, :]
    host_pick = host_member.astype(jnp.bfloat16)
    picked = jnp.einsum(
        "ga,adr->gdr",
        host_pick,
        lax.all_gather(factor_a, "fsdp", axis=1, tiled=True),
        preferred_element_type=jnp.float32,
    ).astype(jnp.bfloat16)
    input_groups = inputs.reshape(GPD, slot_rows, feature_cols)
    input_part = jnp.einsum(
        "gsd,gdr->gsr", input_groups, picked, preferred_element_type=jnp.float32
    )
    low_in = lax.psum(input_part, "tensor")
    host_valid = lax.dynamic_slice_in_dim(row_valid, owner_index * host_rows, host_rows).reshape(
        GPD, slot_rows
    )
    low_in_b = (low_in * host_valid[:, :, None]).astype(jnp.bfloat16)
    low_grad_b = low_grad.astype(jnp.bfloat16).reshape(GPD, slot_rows, rank_dim)
    low_rank = jnp.einsum("gsr,gdr->gsd", low_grad_b, picked, preferred_element_type=jnp.float32)
    input_grad = (base_term + low_rank.reshape(host_rows, feature_cols)).astype(jnp.bfloat16)
    host_grad = jnp.einsum(
        "gsd,gsr->gdr", input_groups, low_grad_b, preferred_element_type=jnp.float32
    )
    spread_grad = jnp.einsum(
        "ga,gdr->adr", host_member.astype(jnp.float32), host_grad, precision=lax.Precision.HIGHEST
    )
    grad_a = lax.psum_scatter(spread_grad, "fsdp", scatter_dimension=1, tiled=True)
    all_inputs = lax.all_gather(low_in_b.reshape(host_rows, rank_dim), "fsdp", axis=0, tiled=True)
    spread_in = (member.astype(jnp.bfloat16)[:, :, None] * all_inputs[:, None, :]).reshape(
        total_rows, adapters * rank_dim
    )
    grad_flat = lax.dot_general(
        spread_in, gathered, (((0,), (0,)), ((), ())), preferred_element_type=jnp.float32
    )
    grad_b = grad_flat.reshape(adapters, rank_dim, hidden_cols).astype(jnp.bfloat16)
    return (input_grad, grad_a, grad_b)


def take(blocks, index):
    return lax.dynamic_index_in_dim(blocks, index, 0, keepdims=False)


def swap(value, axis, mask, count):
    return lax.ppermute(value, axis, [(i, i ^ mask) for i in range(count)])


def after(value, earlier):
    return lax.optimization_barrier((value, earlier))[0]


def body4(inputs, grad_out, base_weight, factor_a, factor_b, group_adapter, group_len):
    n = 4
    host_rows, feature_cols = inputs.shape
    adapters, rank_dim, hidden_cols = factor_b.shape
    own_cols = feature_cols // n
    total_rows = host_rows * n
    slot_rows = total_rows // group_adapter.shape[0]
    t = lax.axis_index("tensor")
    z = lax.axis_index("fsdp")
    wide = adapters * rank_dim
    chunks = 2
    step_rows = host_rows // chunks
    bf16, f32 = jnp.bfloat16, jnp.float32

    mate = swap(grad_out, "tensor", 1, n)
    first = swap(grad_out[:step_rows], "tensor", 2, n)
    first_relayed = swap(first, "tensor", 1, n)

    by_owner = inputs.reshape(host_rows, n, own_cols).transpose(1, 0, 2)
    kept = take(by_owner, z)
    arrived = [kept] + [swap(take(by_owner, z ^ j), "fsdp", j, n) for j in range(1, n)]
    rows_in = jnp.stack(arrived)

    row_index = jnp.arange(total_rows, dtype=jnp.int32)
    adapter_row = jnp.repeat(group_adapter, slot_rows)
    length_row = jnp.repeat(group_len, slot_rows)
    row_valid = (row_index % slot_rows < length_row).astype(f32)
    member = (adapter_row[:, None] == jnp.arange(adapters, dtype=jnp.int32)[None, :]).astype(
        f32
    ) * row_valid[:, None]
    member_blocks = member.reshape(n, host_rows, adapters)

    def ordered(blocks, start):
        return jnp.stack([take(blocks, start ^ j) for j in range(n)])

    def pick(every, who):
        rows = every.shape[0]
        return jnp.sum(every.reshape(rows, adapters, rank_dim) * who[:, :, None], axis=1)

    def spread(low, who):
        rows = low.shape[0]
        return (who.astype(bf16)[:, :, None] * low.astype(bf16)[:, None, :]).reshape(rows, wide)

    b_flat = factor_b.reshape(wide, hidden_cols)
    a_flat = jnp.transpose(factor_a, (1, 0, 2)).reshape(own_cols, wide)
    def doubled(value):
        value = value + swap(value, "fsdp", 1, n)
        return value + swap(value, "fsdp", 2, n)

    def every_block(value, earlier):
        pair = jnp.stack([value, swap(value, "tensor", 1, n)])
        pair = after(pair, earlier)
        return jnp.concatenate([pair, swap(pair, "tensor", 2, n)], axis=0)

    own_member = take(member_blocks, t)
    grad_part = pick(
        lax.dot_general(grad_out, b_flat, (((1,), (1,)), ((), ())), preferred_element_type=f32),
        own_member,
    )
    grad_order = every_block(doubled(grad_part).astype(bf16), first)
    second = swap(after(grad_out[step_rows:], grad_order), "tensor", 2, n)
    low_grad = ordered(grad_order, t).reshape(total_rows, rank_dim)

    rows_in = ordered(rows_in, z).reshape(total_rows, own_cols)
    in_part = pick(jnp.dot(rows_in, a_flat, preferred_element_type=f32), member)
    by_core = in_part.reshape(2, 2, host_rows, rank_dim).transpose(1, 0, 2, 3)
    spread_grad = spread(low_grad, member)
    grad_a = lax.dot_general(
        spread_grad, rows_in, (((0,), (0,)), ((), ())), preferred_element_type=f32
    ).reshape(adapters, rank_dim, own_cols).transpose(0, 2, 1)
    low_rank = lax.dot_general(
        spread_grad, a_flat, (((1,), (1,)), ((), ())), preferred_element_type=f32
    )
    low_rank = lax.dynamic_update_slice_in_dim(
        jnp.zeros((total_rows, feature_cols), bf16), low_rank.astype(bf16), z * own_cols, 1
    ).reshape(n, host_rows, feature_cols)

    member_order = ordered(member_blocks, t)

    grad_b = None
    finished, passed, operands = [], [], []
    for c in range(chunks):
        rows = slice(c * step_rows, (c + 1) * step_rows)
        across, relayed = (first, first_relayed) if c == 0 else (second, second_relayed)
        gathered = jnp.concatenate([grad_out[rows], mate[rows], across, relayed], axis=0)
        if passed:
            gathered = after(gathered, passed[n - 3])
        part = lax.dot_general(
            gathered, base_weight, (((1,), (1,)), ((), ())), preferred_element_type=f32
        ).astype(bf16).reshape(n, step_rows, feature_cols)

        def own(dest, rows=rows, part=part):
            dest = jnp.clip(dest, 0, n - 1)
            return take(part, dest ^ t).astype(f32) + take(low_rank[:, rows], dest).astype(f32)

        operands.append(gathered)
        if c == 0:
            second_relayed = swap(after(second, part), "tensor", 1, n)
            halves = after(by_core, (second, part))
            halves = take(halves, t % 2) + swap(take(halves, 1 - t % 2), "tensor", 1, n)
            own_in = take(halves, t // 2) + swap(take(halves, 1 - t // 2), "tensor", 2, n)
            own_in = doubled(own_in).astype(bf16)
            in_order = every_block(own_in, part)
        up = down = None
        passed = []
        for k in range(1, n):
            to_up, to_down = own(z + n - k), own(z - n + k)
            if up is not None:
                to_up, to_down = to_up + up.astype(f32), to_down + down.astype(f32)
            up = lax.ppermute(to_up.astype(bf16), "fsdp", [(i, i + 1) for i in range(k)])
            down = lax.ppermute(
                to_down.astype(bf16), "fsdp", [(n - 1 - i, n - 2 - i) for i in range(k)]
            )
            if c == chunks - 1 and k > 1:
                rows = slice((k - 2) * step_rows, (k - 1) * step_rows)
                spread_in = spread(
                    in_order[:, rows].reshape(n * step_rows, rank_dim),
                    member_order[:, rows].reshape(n * step_rows, adapters),
                )
                term = lax.dot_general(
                    after(spread_in, passed[-1]),
                    operands[k - 2],
                    (((0,), (0,)), ((), ())),
                    preferred_element_type=f32,
                )
                grad_b = term if grad_b is None else grad_b + term
                if k < n - 1:
                    grad_b, up, down = lax.optimization_barrier((grad_b, up, down))
            passed.append((up, down))
        finished.append((own(z) + up.astype(f32) + down.astype(f32)).astype(bf16))

    grad_b = grad_b.astype(bf16).reshape(adapters, rank_dim, hidden_cols)
    return (jnp.concatenate(finished, axis=0), grad_a, grad_b)


def solution(mesh):
    small = mesh.shape["fsdp"] == 4 and mesh.shape["tensor"] == 4
    placed = (
        P(("group", "fsdp"), "tensor"),
        P(("group", "tensor"), "fsdp"),
        P("tensor", "fsdp"),
        P(None, ("tensor", "fsdp"), None),
        P(None, None, "fsdp"),
        P("group"),
        P("group"),
    )
    return jax.shard_map(
        body4 if small else body,
        mesh=mesh,
        in_specs=placed,
        out_specs=(
            P(("group", "fsdp"), "tensor"),
            P("group", ("tensor", "fsdp"), None),
            P("group", None, "fsdp"),
        ),
        check_vma=False,
    )
```
